256 devices in a mesh: dx: 16 (over z_hi, x, core), dy: 16 (over z_lo, y).
Axes of the slice: x: 4, y: 4, z: 8 (z_hi: 2, z_lo: 4; z = z_hi * 4 + z_lo), core: 2. Of those that a mesh axis runs over, the one named last changes fastest.
Arguments:
- features: bfloat16 [16, 16, 384, 128], P('dx', 'dy'), may hold values from -6 to 6
- positions: bfloat16 [16, 16, 3, 384], P('dx', 'dy'), may hold values from 0 to 1
- atom_count: int32 [16, 16], P('dx', 'dy'), may hold values from 192 to 384, as said below
- ghost_index: int32 [16, 16, 256], P('dx', 'dy'), may hold values from 0 to 383, as said below
- neighbour_list: int32 [16, 16, 384, 32], P('dx', 'dy'), may hold values from 0 to 2687, as said below
- cell_index: int32 [16, 16, 384], P('dx', 'dy'), may hold values from 0 to 65535
- w_self: bfloat16 [128, 128], replicated, may hold values from -0.5 to 0.5
- w_pair: bfloat16 [128, 256], replicated, may hold values from -0.5 to 0.5
- w_radial: float32 [8, 128], replicated, may hold values from -2 to 2
- w_expand: bfloat16 [128, 1024], replicated, may hold values from -0.5 to 0.5
- w_contract: bfloat16 [1024, 128], replicated, may hold values from -0.1875 to 0.1875
- w_final: bfloat16 [128, 128], replicated, may hold values from -0.5 to 0.5
- w_charge: bfloat16 [128], replicated, may hold values from -0.5 to 0.5
Outputs:
- forces: float32 [16, 16, 3, 384], P('dx', 'dy')
The draws below stay inside these ranges and needn't reach their ends.
Inputs may be any that keep to these rules, and one draw needn't show every extreme that they name: `atom_count`: each domain holds at least half of 384 live atoms in its first slots, and some domain is full. `ghost_index`: each entry is a live slot of the same domain. `neighbour_list`: each entry is a live slot of the domain itself or a slot of a ghost block other than block 4 (the domain's own exports).
All inputs are finite; a program needn't handle non-finite values.
Results may differ from the reference program's by a relative error of at most 0.0049.
Values may be sent and summed in bfloat16 or wider, within the bound.
A program may use at most 128 MiB of HBM per device.

```python
import math
import jax
import jax.numpy as jnp
from jax import lax

WIDTH = 128
LATENT = 1024
BASIS = 8
NEIGHBOURS = 32
ATOM_BLOCK = 64
ATOMS = 384
GHOSTS = 256
GRID_X = 8
GRID_Y = 8
GRID_Z = 1024
N_DX = 16
N_DY = 16


def live_counts(key):
    sub = jax.random.fold_in(key, 11)
    first, second = jax.random.split(sub)
    base = jax.random.randint(first, (N_DX * N_DY,), ATOMS // 2, ATOMS + 1)
    chosen = jax.random.randint(second, (), 0, N_DX * N_DY)
    filled = jnp.where(jnp.arange(N_DX * N_DY) == chosen, ATOMS, base)
    return filled.reshape(N_DX, N_DY).astype(jnp.int32)


def draw_atom_count(key, part):
    return live_counts(key)


def draw_ghost_index(key, part):
    counts = live_counts(key)
    sub = jax.random.fold_in(key, 12)
    return jax.random.randint(sub, (N_DX, N_DY, GHOSTS), 0, counts[:, :, None]).astype(jnp.int32)


def draw_neighbour_list(key, part):
    counts = live_counts(key)
    sub = jax.random.fold_in(key, 13)
    key_local, key_block, key_slot, key_side = jax.random.split(sub, 4)
    shape = (N_DX, N_DY, ATOMS, NEIGHBOURS)
    local_slot = jax.random.randint(key_local, shape, 0, counts[:, :, None, None])
    which = jax.random.randint(key_block, shape, 0, 8)
    block_id = which + (which >= 4).astype(jnp.int32)
    ghost_slot = jax.random.randint(key_slot, shape, 0, GHOSTS)
    ghost_entry = ATOMS + block_id * GHOSTS + ghost_slot
    side = jax.random.randint(key_side, shape, 0, 2)
    result = jnp.where(side == 0, local_slot, ghost_entry).astype(jnp.int32)
    result = result.at[0, 0, 0, 0].set(0)
    result = result.at[0, 0, 0, 1].set(ATOMS + 9 * GHOSTS - 1)
    return result.astype(jnp.int32)


def with_ends(drawn, key, least, top_value):
    longest = drawn.shape.index(max(drawn.shape))
    spots = []
    for shift in (0, 1):
        where = [jax.random.randint(jax.random.fold_in(key, axis), (), 0, length) for axis, length in enumerate(drawn.shape)]
        where[longest] = (where[longest] + shift) % drawn.shape[longest]
        spots.append(tuple(where))
    return drawn.at[spots[0]].set(least).at[spots[1]].set(top_value)


def block_levels(rng, extent, shards, low, largest):
    gain = 1.0
    for dim, parts in shards:
        draws = jax.random.uniform(jax.random.fold_in(jax.random.fold_in(rng, 6), dim), (parts,), jnp.float32, low / len(shards), largest / len(shards))
        gain = gain * jnp.repeat(jnp.exp(draws), extent[dim] // parts).reshape((-1,) + (1,) * (len(extent) - 1 - dim))
    return gain


def bell_draw(key, shape, scale, limit, cuts=(), kind=jnp.bfloat16):
    drawn = jax.random.normal(key, shape, jnp.float32) * scale
    if len(cuts) > 0:
        drawn = block_levels(key, shape, cuts, -0.22, 0.18) * drawn
    return jnp.clip(drawn, min=-limit, max=limit).astype(kind)


def setup_inputs(seed: int = 0) -> dict:
    keys = jax.random.split(jax.random.key(seed), 14)
    return {
        "features": bell_draw(keys[0], (N_DX, N_DY, ATOMS, WIDTH), 1.0, 6.0, ((0, 16), (1, 16))),
        "positions": jnp.clip(1.0 * jax.random.uniform(keys[1], (N_DX, N_DY, 3, ATOMS), jnp.float32) ** block_levels(keys[1], (N_DX, N_DY, 3, ATOMS), ((0, 16), (1, 16)), -0.2, 0.2), 0.0, 1.0).astype(jnp.bfloat16),
        "atom_count": draw_atom_count(jax.random.fold_in(keys[13], 71), 0),
        "ghost_index": draw_ghost_index(jax.random.fold_in(keys[13], 71), 0),
        "neighbour_list": draw_neighbour_list(jax.random.fold_in(keys[13], 71), 0),
        "cell_index": with_ends(jax.random.randint(keys[5], (N_DX, N_DY, ATOMS), 0, GRID_X * GRID_Y * GRID_Z), jax.random.fold_in(keys[5], 1), 0, (GRID_X * GRID_Y * GRID_Z) - 1).astype(jnp.int32),
        "w_self": bell_draw(keys[6], (WIDTH, WIDTH), WIDTH ** -0.5, 0.5),
        "w_pair": bell_draw(keys[7], (WIDTH, 2 * WIDTH), WIDTH ** -0.5, 0.5),
        "w_radial": bell_draw(keys[8], (BASIS, WIDTH), BASIS ** -0.5, 2.0, (), jnp.float32),
        "w_expand": bell_draw(keys[9], (WIDTH, LATENT), WIDTH ** -0.5, 0.5),
        "w_contract": bell_draw(keys[10], (LATENT, WIDTH), LATENT ** -0.5, 0.1875),
        "w_final": bell_draw(keys[11], (WIDTH, WIDTH), WIDTH ** -0.5, 0.5),
        "w_charge": bell_draw(keys[12], (WIDTH,), WIDTH ** -0.5, 0.5),
    }


box_side = 1.0
cutoff_sq = 6.25
smearing = 1.0

def short_range(features, projected, own_coords, ext_coords, block_lists_all, w_self, w_radial, w_expand, w_contract, w_final):
    channels = features.shape[1]
    atom_rows = features.shape[0]
    per_atom = block_lists_all.shape[1]
    basis_count = w_radial.shape[0]
    block_count = atom_rows // ATOM_BLOCK
    own_term = jnp.dot(features, w_self, preferred_element_type=jnp.float32)
    spacing = cutoff_sq / (basis_count - 1)
    centers = jnp.arange(basis_count, dtype=jnp.float32) * spacing
    edge_scale = 1.0 / math.sqrt(per_atom)

    def one_block(inputs):
        own_rows, near_coords, block_lists = inputs
        flat_list = block_lists.reshape(-1)
        gathered = jnp.take(projected, flat_list, axis=0)
        bias_rows = gathered[:, :channels].astype(jnp.float32)
        value_rows = gathered[:, channels:].astype(jnp.float32)
        far_coords = jnp.take(ext_coords, flat_list, axis=1)
        start_coords = jnp.broadcast_to(near_coords[:, :, None], (3, near_coords.shape[1], per_atom)).reshape(3, -1)
        displace = far_coords - start_coords
        dist_sq = lax.optimization_barrier(jnp.sum(displace * displace, axis=0))
        basis_rows = jnp.exp(-jnp.square((dist_sq[None, :] - centers[:, None]) / spacing))
        envelope = jnp.square(jnp.maximum(0.0, 1.0 - dist_sq / cutoff_sq))
        radial = lax.dot_general(basis_rows, w_radial, (((0,), (0,)), ((), ())), precision=lax.Precision.HIGHEST, preferred_element_type=jnp.float32)
        own_edges = jnp.broadcast_to(own_rows[:, None, :], (own_rows.shape[0], per_atom, channels)).reshape(-1, channels)
        edge_in = jax.nn.silu(radial + own_edges + bias_rows).astype(jnp.bfloat16)
        latent = jax.nn.silu(jnp.dot(edge_in, w_expand, preferred_element_type=jnp.float32)).astype(jnp.bfloat16)
        mixed_out = jnp.dot(latent, w_contract, preferred_element_type=jnp.float32)
        weight = mixed_out * envelope[:, None] * value_rows
        scalar = weight.reshape(-1, per_atom, channels).sum(axis=1) * edge_scale
        vector = (displace[:, :, None] * weight[None]).reshape(3, -1, per_atom, channels).sum(axis=2) * edge_scale
        invariant = (scalar + lax.optimization_barrier(jnp.sum(vector * vector, axis=0)) / 3.0).astype(jnp.bfloat16)
        gating = jax.nn.silu(jnp.dot(invariant, w_final, preferred_element_type=jnp.float32))
        return lax.optimization_barrier(jnp.sum(vector * gating[None], axis=2)) / math.sqrt(channels)
    own_blocks = own_term.reshape(block_count, ATOM_BLOCK, channels)
    coord_blocks = own_coords.reshape(3, block_count, ATOM_BLOCK).transpose(1, 0, 2)
    list_blocks = block_lists_all.reshape(block_count, ATOM_BLOCK, per_atom)
    result = lax.map(one_block, (own_blocks, coord_blocks, list_blocks))
    return result.transpose(1, 0, 2).reshape(3, atom_rows)

def signed_modes(count):
    modes = jnp.arange(count, dtype=jnp.int32)
    return jnp.where(modes < count // 2, modes, modes - count)

def reference(features, positions, atom_count, ghost_index, neighbour_list, cell_index, w_self, w_pair, w_radial, w_expand, w_contract, w_final, w_charge):
    exported_feat = jnp.take_along_axis(features, ghost_index[:, :, :, None], axis=2)
    exported_coords = jnp.take_along_axis(positions, ghost_index[:, :, None, :], axis=3).astype(jnp.float32)
    feat_blocks = []
    coord_blocks = []
    for shift_x in range(3):
        for shift_y in range(3):
            moved_feat = jnp.roll(exported_feat, (1 - shift_x, 1 - shift_y), axis=(0, 1))
            moved_coords = jnp.roll(exported_coords, (1 - shift_x, 1 - shift_y), axis=(0, 1))
            offsets = jnp.array([(shift_x - 1) * box_side, (shift_y - 1) * box_side, 0.0], dtype=jnp.float32)
            feat_blocks.append(moved_feat)
            coord_blocks.append(moved_coords + offsets[None, None, :, None])
    ghost_feat = jnp.stack(feat_blocks, axis=2).reshape(N_DX, N_DY, 9 * GHOSTS, WIDTH)
    ghost_coords = jnp.stack(coord_blocks, axis=3).reshape(N_DX, N_DY, 3, 9 * GHOSTS)
    own_coords = positions.astype(jnp.float32)
    ext_feat = jnp.concatenate([features, ghost_feat], axis=2)
    ext_coords = jnp.concatenate([own_coords, ghost_coords], axis=3)
    devices_all = N_DX * N_DY

    def per_domain(inputs):
        feat_one, ext_one, coords_one, ext_coords_one, lists_one = inputs
        projected = jnp.dot(ext_one, w_pair, preferred_element_type=jnp.float32).astype(jnp.bfloat16)
        return short_range(feat_one, projected, coords_one, ext_coords_one, lists_one, w_self, w_radial, w_expand, w_contract, w_final)
    short = lax.map(per_domain, (features.reshape(devices_all, ATOMS, WIDTH), ext_feat.reshape(devices_all, ATOMS + 9 * GHOSTS, WIDTH), own_coords.reshape(devices_all, 3, ATOMS), ext_coords.reshape(devices_all, 3, ATOMS + 9 * GHOSTS), neighbour_list.reshape(devices_all, ATOMS, NEIGHBOURS))).reshape(N_DX, N_DY, 3, ATOMS)
    live = jnp.arange(ATOMS, dtype=jnp.int32)[None, None, :] < atom_count[:, :, None]
    charge = lax.optimization_barrier(jnp.sum(features.astype(jnp.float32) * w_charge.astype(jnp.float32), axis=-1))
    charge = jnp.where(live, charge, jnp.zeros_like(charge))
    mesh_x = GRID_X * N_DX
    mesh_y = GRID_Y * N_DY
    local_x = cell_index // (GRID_Y * GRID_Z)
    local_y = cell_index // GRID_Z % GRID_Y
    local_z = cell_index % GRID_Z
    row_dev = jnp.arange(N_DX, dtype=jnp.int32)[:, None, None]
    col_dev = jnp.arange(N_DY, dtype=jnp.int32)[None, :, None]
    global_flat = ((row_dev * GRID_X + local_x) * mesh_y + col_dev * GRID_Y + local_y) * GRID_Z + local_z
    density = jax.ops.segment_sum(charge.reshape(-1), global_flat.reshape(-1).astype(jnp.int32), num_segments=mesh_x * mesh_y * GRID_Z)
    density = density.reshape(mesh_x, mesh_y, GRID_Z)
    sig_x = signed_modes(mesh_x)[:, None, None]
    sig_y = signed_modes(mesh_y)[None, :, None]
    sig_z = signed_modes(GRID_Z)[None, None, :]
    wave_x = sig_x.astype(jnp.float32) * (2.0 * math.pi / mesh_x)
    wave_y = sig_y.astype(jnp.float32) * (2.0 * math.pi / mesh_y)
    wave_z = sig_z.astype(jnp.float32) * (2.0 * math.pi / GRID_Z)
    wave_sq = wave_x * wave_x + wave_y * wave_y + wave_z * wave_z
    is_zero = (sig_x == 0) & (sig_y == 0) & (sig_z == 0)
    safe_sq = jnp.where(is_zero, jnp.ones_like(wave_sq), wave_sq)
    green = jnp.where(is_zero, jnp.zeros_like(wave_sq), 4.0 * math.pi * jnp.exp(-0.5 * smearing * smearing * wave_sq) / safe_sq)
    spectrum = jnp.fft.fftn(density) * green
    derivatives = []
    for signed, wave, count in ((sig_x, wave_x, mesh_x), (sig_y, wave_y, mesh_y), (sig_z, wave_z, GRID_Z)):
        derivatives.append(jnp.where(signed * 2 == -count, jnp.zeros_like(wave), wave))
    samples = []
    for wave in derivatives:
        field = jnp.real(jnp.fft.ifftn(-1j * wave * spectrum))
        samples.append(jnp.take(field.reshape(-1), global_flat.reshape(-1).astype(jnp.int32)).reshape(N_DX, N_DY, ATOMS))
    sampled = jnp.stack(samples, axis=2)
    total = short + charge[:, :, None, :] * sampled
    return jnp.where(live[:, :, None, :], total, jnp.zeros_like(total))
```

```python
import functools
import math

import numpy as np
import ml_dtypes

import jax
import jax.numpy as jnp
from jax import lax
from jax.experimental import pallas as pl
from jax.experimental.pallas import tpu as pltpu
from jax.sharding import PartitionSpec as P

F32 = jnp.float32
BF = jnp.bfloat16
MESH = pl.DeviceIdType.MESH

SIDE = 16
ATOMS = 384
GHOSTS = 256
SLOTS = 32
GROUP = 16
EDGES = GROUP * SLOTS
BLOCKS = ATOMS // GROUP
EXT = ATOMS + 9 * GHOSTS
CUT = 6.25


def real_basis(count):
    n = np.arange(count)
    rows = np.zeros((count, count))
    slope = np.zeros((count, count))
    rows[0] = 1.0 / math.sqrt(count)
    rows[1] = np.where(n % 2 == 0, 1.0, -1.0) / math.sqrt(count)
    for k in range(1, count // 2):
        angle = 2.0 * math.pi * (k * n % count) / count
        rows[2 * k] = math.sqrt(2.0 / count) * np.cos(angle)
        rows[2 * k + 1] = math.sqrt(2.0 / count) * np.sin(angle)
        wave = 2.0 * math.pi * k / count
        slope[2 * k] = wave * rows[2 * k + 1]
        slope[2 * k + 1] = -wave * rows[2 * k]
    return rows, slope


def halves(table):
    high = table.astype(np.float32).astype(ml_dtypes.bfloat16)
    low = (table - high.astype(np.float64)).astype(np.float32).astype(ml_dtypes.bfloat16)
    return np.stack([high, low])


def grid_tables():
    basis, slope = real_basis(8 * SIDE)
    eye = np.eye(4)
    by = basis.reshape(SIDE, 2, 4, SIDE, 8)
    dy = slope.reshape(SIDE, 2, 4, SIDE, 8)
    y_forward = np.einsum("phkry,ab->hpkarby", by, eye).reshape(512, 512)
    y_back = np.stack(
        [
            np.einsum("phkry,ab->rayhpkb", by, eye),
            np.einsum("phkry,ab->rayhpkb", dy, eye),
        ]
    ).reshape(1024, 512)
    bx = basis.reshape(128, SIDE, 2, 4)
    dx = slope.reshape(128, SIDE, 2, 4)
    x_forward = np.einsum("sphx,ab->sapbhx", bx, eye)
    x_forward = x_forward.transpose(0, 1, 2, 4, 3, 5).reshape(512, 512)
    x_back = np.einsum("fsphx,ab->pfhbxsa", np.stack([bx, dx]), eye)
    x_back = x_back.reshape(1024, 512)
    z = np.arange(1024)
    coarse = 2.0 * math.pi * (32 * np.arange(16)[:, None] * z % 1024) / 1024
    fine = 2.0 * math.pi * (np.arange(32)[:, None] * z % 1024) / 1024
    scale = math.sqrt(2.0 / 1024)
    z_rows = np.concatenate(
        [np.cos(coarse), np.sin(coarse), scale * np.cos(fine), scale * np.sin(fine)]
    )
    return tuple(halves(t) for t in (y_forward, x_forward, x_back, y_back, z_rows))


def silu(x):
    half = 0.5 * x
    return half + half * jnp.tanh(half)


def transposed_left(a, b):
    return lax.dot_general(a, b, (((0,), (0,)), ((), ())), preferred_element_type=F32)


def transposed_right(a, b):
    return lax.dot_general(a, b, (((1,), (1,)), ((), ())), preferred_element_type=F32)


def fill_table(table, first, count, feat, pos, w_pair, shift_x, shift_y):
    flat = table.reshape(EXT * 8, 128)
    projected = jnp.dot(feat, w_pair, preferred_element_type=F32).astype(BF).astype(F32)
    lane = lax.broadcasted_iota(jnp.int32, (16, 384), 1)
    row = lax.broadcasted_iota(jnp.int32, (16, 384), 0)
    spread = (lane // 128 == row).astype(F32).astype(BF)
    xyz = transposed_left(pos, spread)
    parts = (
        projected[:, :128],
        projected[:, 128:],
        xyz[:, :128] + shift_x,
        xyz[:, 128:256] + shift_y,
        xyz[:, 256:],
    )
    for k, part in enumerate(parts):
        flat[pl.ds(first * 8 + k, count, stride=8), :] = part


def gather_edges(block, lists, table, picked, unroll):
    def one_slot(k, carry):
        for a in range(GROUP):
            j = lists[block * GROUP + a, k]
            picked[k * GROUP + a] = table[j]
        return carry

    lax.fori_loop(0, SLOTS, one_slot, 0, unroll=unroll)


def edge_block(block, table, picked, own, radial_w, expand_w, contract_w, sums):
    first = pl.multiple_of(block * GROUP, GROUP)
    picked = picked.reshape(EDGES * 8, 128)
    table = table.reshape(EXT * 8, 128)

    def far(k):
        return picked[pl.ds(k, EDGES, stride=8), :].reshape(SLOTS, GROUP, 128)

    def near(k):
        return table[pl.ds(first * 8 + k, GROUP, stride=8), :][None]

    dx, dy, dz = far(2) - near(2), far(3) - near(3), far(4) - near(4)
    d2 = dx * dx + dy * dy + dz * dz
    lane = lax.broadcasted_iota(jnp.int32, (1, 1, 128), 2)
    u = d2 * (7.0 / CUT) - (lane % 8).astype(F32)
    basis = jnp.exp(-(u * u))
    envelope = jnp.square(jnp.maximum(0.0, 1.0 - d2 * (1.0 / CUT)))
    rest = basis - basis.astype(BF).astype(F32)
    left = jnp.where((lane >= 8) & (lane < 16), rest, basis).astype(BF)
    radial = jnp.dot(
        left.reshape(EDGES, 128), radial_w[...], preferred_element_type=F32
    ).reshape(SLOTS, GROUP, 128)
    edge_in = silu(radial + own[pl.ds(first, GROUP), :][None] + far(0))
    edge_in = edge_in.astype(BF).reshape(EDGES, 128)
    half = jnp.dot(edge_in, expand_w[...], preferred_element_type=F32)
    latent = (half + half * jnp.tanh(half)).astype(BF)
    mixed = jnp.dot(latent, contract_w[...], preferred_element_type=F32)
    weight = mixed.reshape(SLOTS, GROUP, 128) * envelope * far(1)
    scale = 1.0 / math.sqrt(SLOTS)
    for i, term in enumerate((weight, dx * weight, dy * weight, dz * weight)):
        sums[i, pl.ds(first, GROUP), :] = jnp.sum(term, axis=0) * scale


def edge_forces(sums, w_final):
    scalar, vx, vy, vz = (sums[i] for i in range(4))
    invariant = (scalar + (vx * vx + vy * vy + vz * vz) / 3.0).astype(BF)
    gate = silu(jnp.dot(invariant, w_final, preferred_element_type=F32))
    ones = jnp.ones((8, 128), F32)
    rows = [
        lax.dot_general(
            ones,
            v * gate,
            (((1,), (1,)), ((), ())),
            precision=lax.Precision.HIGHEST,
            preferred_element_type=F32,
        )[0:1]
        for v in (vx, vy, vz)
    ]
    return [row * (1.0 / math.sqrt(128.0)) for row in rows]


def two_halves(table, right):
    return jnp.dot(table[0], right, preferred_element_type=F32) + jnp.dot(
        table[1], right, preferred_element_type=F32
    )


def swap_halves(low, high):
    lane = lax.broadcasted_iota(jnp.int32, low.shape, low.ndim - 1)
    first = lane < 64
    turned_high = pltpu.roll(high, 64, high.ndim - 1)
    turned_low = pltpu.roll(low, 64, low.ndim - 1)
    return jnp.where(first, low, turned_high), jnp.where(first, turned_low, high)


def green_block(px, ry):
    row = lax.broadcasted_iota(jnp.int32, (512, 128), 0)
    lane = lax.broadcasted_iota(jnp.int32, (512, 128), 1)
    x_slot = row // 4
    y_slot = px * 8 + (lane // 64) * 4 + row % 4
    c = lane % 64
    x_mode = jnp.where(x_slot == 1, 64, x_slot // 2)
    y_mode = jnp.where(y_slot == 1, 64, y_slot // 2)
    z_mode = jnp.where((c == 32) & (ry == 0), 512, ry * 32 + c % 32)
    kx = x_mode.astype(F32) * (2.0 * math.pi / 128)
    ky = y_mode.astype(F32) * (2.0 * math.pi / 128)
    kz = z_mode.astype(F32) * (2.0 * math.pi / 1024)
    kk = kx * kx + ky * ky + kz * kz
    zero = (x_mode == 0) & (y_mode == 0) & (z_mode == 0)
    safe = jnp.where(zero, 1.0, kk)
    return jnp.where(zero, 0.0, 4.0 * math.pi * jnp.exp(-0.5 * kk) / safe)


class Exchange:
    def __init__(self, axis, outgoing, landing, send_sems, recv_sems):
        self.axis = axis
        self.outgoing, self.landing = outgoing, landing
        self.send_sems, self.recv_sems = send_sems, recv_sems
        self.me = lax.axis_index(axis)

    def copy(self, step, target, slot):
        return pltpu.make_async_remote_copy(
            src_ref=self.outgoing.at[target],
            dst_ref=self.landing.at[slot],
            send_sem=self.send_sems.at[step],
            recv_sem=self.recv_sems.at[step],
            device_id={self.axis: target},
            device_id_type=MESH,
        )

    def start(self):
        def one(step, carry):
            target = lax.rem(self.me + step, SIDE)
            self.copy(step, target, self.me).start()
            return carry

        lax.fori_loop(1, SIDE, one, 0)
        self.landing[pl.ds(self.me, 1)] = self.outgoing[pl.ds(self.me, 1)]

    def wait_recv(self):
        def one(step, carry):
            target = lax.rem(self.me + step, SIDE)
            source = lax.rem(self.me - step + SIDE, SIDE)
            self.copy(step, target, source).wait_recv()
            return carry

        lax.fori_loop(1, SIDE, one, 0)

    def wait_send(self):
        def one(step, carry):
            target = lax.rem(self.me + step, SIDE)
            self.copy(step, target, self.me).wait_send()
            return carry

        lax.fori_loop(1, SIDE, one, 0)


GHOST_BLOCKS = tuple(b for b in range(9) if b != 4)


def device_kernel(
    lists,
    count,
    feat,
    positions,
    exports,
    cells,
    w_self,
    w_pair,
    w_radial,
    w_expand,
    w_contract,
    w_final,
    w_charge,
    y_forward,
    x_forward,
    x_back,
    y_back,
    z_rows,
    out,
    table,
    picked_even,
    picked_odd,
    own,
    radial_w,
    expand_w,
    sums,
    pos16,
    out_feat,
    out_pos,
    ghost_feat,
    ghost_pos,
    z_basis,
    send1,
    land1,
    send2,
    land2,
    send3,
    land3,
    send4,
    land4,
    sems,
    halo_sems,
):
    px = lax.axis_index("dx")
    ry = lax.axis_index("dy")
    barrier = pltpu.get_barrier_semaphore()

    def greet(step, carry):
        pl.semaphore_signal(
            barrier,
            inc=1,
            device_id={"dx": lax.rem(px + step, SIDE), "dy": ry},
            device_id_type=MESH,
        )
        pl.semaphore_signal(
            barrier,
            inc=1,
            device_id={"dx": px, "dy": lax.rem(ry + step, SIDE)},
            device_id_type=MESH,
        )
        return carry

    lax.fori_loop(1, SIDE, greet, 0)
    for a in (1, SIDE - 1):
        for b in (1, SIDE - 1):
            pl.semaphore_signal(
                barrier,
                inc=1,
                device_id={"dx": lax.rem(px + a, SIDE), "dy": lax.rem(ry + b, SIDE)},
                device_id_type=MESH,
            )

    pos16[...] = jnp.zeros_like(pos16)
    pos16[0:3, :] = positions[...].astype(F32)
    pos = pos16[...].astype(BF)
    slot = lax.broadcasted_iota(jnp.int32, (ATOMS, GHOSTS), 0)
    chosen = (slot == exports[...]).astype(F32).astype(BF)
    out_feat[...] = transposed_left(chosen, feat[...]).astype(BF)
    out_pos[...] = jnp.dot(pos, chosen, preferred_element_type=F32).astype(BF)

    cell = cells[...]
    height = cell % 1024
    column = cell // 1024
    level = lax.broadcasted_iota(jnp.int32, (1024, ATOMS), 0)
    at_height = (level == height).astype(F32).astype(BF)
    angles = two_halves(z_rows, at_height)
    fine_cos, fine_sin = angles[32:64], angles[64:96]
    root = math.sqrt(0.5)
    fine_row = lax.broadcasted_iota(jnp.int32, (32, ATOMS), 0)
    alternate = jnp.where(height % 2 == 0, 1.0, -1.0) * math.sqrt(1.0 / 1024)
    for r in range(SIDE):
        big_cos, big_sin = angles[r : r + 1], angles[16 + r : 17 + r]
        cosine = big_cos * fine_cos - big_sin * fine_sin
        sine = big_sin * fine_cos + big_cos * fine_sin
        if r == 0:
            cosine = jnp.where(fine_row == 0, cosine * root, cosine)
            sine = jnp.where(fine_row == 0, alternate, sine)
        z_basis[64 * r : 64 * r + 32, :] = cosine
        z_basis[64 * r + 32 : 64 * r + 64, :] = sine

    charge_w = jnp.broadcast_to(w_charge[...], (8, 128))
    atom = lax.broadcasted_iota(jnp.int32, (1, ATOMS), 1)
    live = atom < count[0, 0]
    charge = jnp.where(live, transposed_right(charge_w, feat[...])[0:1], 0.0)
    place = lax.broadcasted_iota(jnp.int32, (64, ATOMS), 0)
    at_column = (place == column).astype(F32).astype(BF)
    loaded = z_basis[...] * charge
    loaded_high = loaded.astype(BF)
    loaded_low = (loaded - loaded_high.astype(F32)).astype(BF)
    density = transposed_right(at_column, loaded_high) + transposed_right(at_column, loaded_low)
    for q in range(8):
        part = density[:, 128 * q : 128 * q + 128]
        even, odd = swap_halves(part[:32], part[32:])
        send1[2 * q] = even.astype(BF)
        send1[2 * q + 1] = odd.astype(BF)

    pl.semaphore_wait(barrier, 34)
    over_y = Exchange("dy", send1, land1, sems.at[0], sems.at[1])
    over_x = Exchange("dx", send2, land2, sems.at[2], sems.at[3])
    back_x = Exchange("dx", send3, land3, sems.at[4], sems.at[5])
    back_y = Exchange("dy", send4, land4, sems.at[6], sems.at[7])
    over_y.start()
    halo = []
    for i, b in enumerate(GHOST_BLOCKS):
        target = {
            "dx": lax.rem(px + SIDE + 1 - b // 3, SIDE),
            "dy": lax.rem(ry + SIDE + 1 - b % 3, SIDE),
        }
        for j, (source, landing) in enumerate(((out_feat, ghost_feat), (out_pos, ghost_pos))):
            copy = pltpu.make_async_remote_copy(
                src_ref=source,
                dst_ref=landing.at[b],
                send_sem=halo_sems.at[j, i],
                recv_sem=halo_sems.at[2 + j, i],
                device_id=target,
                device_id_type=MESH,
            )
            copy.start()
            halo.append(copy)

    w_rad = w_radial[...]
    rad_high = w_rad.astype(BF).astype(F32)
    stacked = jnp.concatenate(
        [rad_high, rad_high, w_rad - rad_high, jnp.zeros((104, 128), F32)], axis=0
    )
    radial_w[...] = stacked.astype(BF)
    expand_w[...] = (w_expand[...].astype(F32) * 0.5).astype(BF)
    own[...] = jnp.dot(feat[...], w_self[...], preferred_element_type=F32)
    fill_table(table, 0, ATOMS, feat[...], pos, w_pair[...], 0.0, 0.0)
    green = green_block(px, ry)

    over_y.wait_recv()
    along_y = two_halves(y_forward, land1[...].reshape(512, 128))
    low, high = swap_halves(along_y[:256], along_y[256:])
    send2[:, 0:16, :] = low.astype(BF).reshape(SIDE, 16, 128)
    send2[:, 16:32, :] = high.astype(BF).reshape(SIDE, 16, 128)
    over_x.start()

    for copy in halo:
        copy.wait_recv()
    for b in GHOST_BLOCKS:
        fill_table(
            table,
            ATOMS + GHOSTS * b,
            GHOSTS,
            ghost_feat[b],
            ghost_pos[b],
            w_pair[...],
            b // 3 - 1.0,
            b % 3 - 1.0,
        )

    def edges(start, stop):
        fixed = (own, radial_w, expand_w, w_contract, sums)

        def pair(h, carry):
            block = 2 * h
            gather_edges(block + 1, lists, table, picked_odd, SLOTS)
            edge_block(block, table, picked_even, *fixed)
            following = jnp.minimum(block + 2, BLOCKS - 1)
            gather_edges(following, lists, table, picked_even, SLOTS)
            edge_block(block + 1, table, picked_odd, *fixed)
            return carry

        lax.fori_loop(start // 2, stop // 2, pair, 0)

    over_x.wait_recv()
    spectrum = two_halves(x_forward, land2[...].reshape(512, 128)) * green
    top = spectrum.astype(BF)
    rest = (spectrum - top.astype(F32)).astype(BF)
    along_x = two_halves(x_back, top) + jnp.dot(x_back[0], rest, preferred_element_type=F32)
    send3[...] = along_x.astype(BF).reshape(SIDE, 64, 128)
    back_x.start()
    gather_edges(0, lists, table, picked_even, 1)
    edges(0, BLOCKS // 3)

    back_x.wait_recv()
    arrived = []
    for f in range(2):
        low = land3[:, 32 * f : 32 * f + 16, :].astype(F32).reshape(256, 128)
        high = land3[:, 32 * f + 16 : 32 * f + 32, :].astype(F32).reshape(256, 128)
        low, high = swap_halves(low, high)
        arrived.append(jnp.concatenate([low, high], axis=0).astype(BF))
    from_potential = two_halves(y_back, arrived[0]).astype(BF).reshape(2, SIDE, 32, 128)
    from_slope = (
        jnp.dot(y_back[0, 0:512], arrived[1], preferred_element_type=F32)
        + jnp.dot(y_back[1, 0:512], arrived[1], preferred_element_type=F32)
    )
    send4[:, 0:32, :] = from_potential[0]
    send4[:, 32:64, :] = from_slope.astype(BF).reshape(SIDE, 32, 128)
    send4[:, 64:96, :] = from_potential[1]
    back_y.start()
    edges(BLOCKS // 3, BLOCKS)
    short = edge_forces(sums, w_final[...])

    back_y.wait_recv()
    fields = []
    for f in range(3):
        lows, highs = [], []
        for q in range(8):
            low, high = swap_halves(
                land4[2 * q, 32 * f : 32 * f + 32, :].astype(F32),
                land4[2 * q + 1, 32 * f : 32 * f + 32, :].astype(F32),
            )
            lows.append(low)
            highs.append(high)
        coefficients = jnp.concatenate(
            [jnp.concatenate(lows, axis=1), jnp.concatenate(highs, axis=1)], axis=0
        ).astype(BF)
        fields.append(transposed_left(coefficients, at_column))
    potential, slope_x, slope_y = fields
    values = z_basis[...]
    field_x = jnp.sum(slope_x * values, axis=0, keepdims=True)
    field_y = jnp.sum(slope_y * values, axis=0, keepdims=True)
    pairs = potential.reshape(SIDE, 64, ATOMS)
    basis = values.reshape(SIDE, 64, ATOMS)
    wave = (
        lax.broadcasted_iota(jnp.int32, (SIDE, 32, ATOMS), 0) * 32
        + lax.broadcasted_iota(jnp.int32, (SIDE, 32, ATOMS), 1)
    ).astype(F32) * (2.0 * math.pi / 1024)
    turned = wave * (pairs[:, :32] * basis[:, 32:] - pairs[:, 32:] * basis[:, :32])
    field_z = jnp.sum(turned.reshape(512, ATOMS), axis=0, keepdims=True)
    for a, field in enumerate((field_x, field_y, field_z)):
        out[a : a + 1, :] = jnp.where(live, short[a] + charge * field, 0.0)

    for copy in halo:
        copy.wait_send()
    for exchange in (over_y, over_x, back_x, back_y):
        exchange.wait_send()


def shards(
    features,
    positions,
    atom_count,
    ghost_index,
    neighbour_list,
    cell_index,
    w_self,
    w_pair,
    w_radial,
    w_expand,
    w_contract,
    w_final,
    w_charge,
):
    tables = [jnp.asarray(t) for t in grid_tables()]
    vmem = pl.BlockSpec(memory_space=pltpu.VMEM)
    smem = pl.BlockSpec(memory_space=pltpu.SMEM)
    forces = pl.pallas_call(
        device_kernel,
        out_shape=jax.ShapeDtypeStruct((3, ATOMS), F32),
        in_specs=[smem, smem] + [vmem] * 16,
        out_specs=vmem,
        scratch_shapes=[
            pltpu.VMEM((EXT, 8, 128), F32),
            pltpu.VMEM((EDGES, 8, 128), F32),
            pltpu.VMEM((EDGES, 8, 128), F32),
            pltpu.VMEM((ATOMS, 128), F32),
            pltpu.VMEM((128, 128), BF),
            pltpu.VMEM((128, 1024), BF),
            pltpu.VMEM((4, ATOMS, 128), F32),
            pltpu.VMEM((16, ATOMS), F32),
            pltpu.VMEM((GHOSTS, 128), BF),
            pltpu.VMEM((16, GHOSTS), BF),
            pltpu.VMEM((9, GHOSTS, 128), BF),
            pltpu.VMEM((9, 16, GHOSTS), BF),
            pltpu.VMEM((1024, ATOMS), F32),
            pltpu.VMEM((SIDE, 32, 128), BF),
            pltpu.VMEM((SIDE, 32, 128), BF),
            pltpu.VMEM((SIDE, 32, 128), BF),
            pltpu.VMEM((SIDE, 32, 128), BF),
            pltpu.VMEM((SIDE, 64, 128), BF),
            pltpu.VMEM((SIDE, 64, 128), BF),
            pltpu.VMEM((SIDE, 96, 128), BF),
            pltpu.VMEM((SIDE, 96, 128), BF),
            pltpu.SemaphoreType.DMA((8, SIDE)),
            pltpu.SemaphoreType.DMA((4, 8)),
        ],
        compiler_params=pltpu.CompilerParams(
            collective_id=0, has_side_effects=True, vmem_limit_bytes=58 * 2**20
        ),
        name="forces",
    )(
        neighbour_list[0, 0],
        atom_count,
        features[0, 0],
        positions[0, 0],
        ghost_index[0],
        cell_index[0],
        w_self,
        w_pair,
        w_radial,
        w_expand,
        w_contract,
        w_final,
        w_charge[None],
        *tables,
    )
    return forces[None, None]


def solution(mesh):
    whole = P()
    placed = (
        P("dx", "dy", None, None),
        P("dx", "dy", None, None),
        P("dx", "dy"),
        P("dx", "dy", None),
        P("dx", "dy", None, None),
        P("dx", "dy", None),
    ) + (whole,) * 7
    return jax.shard_map(
        shards, mesh=mesh, in_specs=placed, out_specs=P("dx", "dy", None, None), check_vma=False
    )
```

```python
import functools
import math

import numpy as np
import ml_dtypes

import jax
import jax.numpy as jnp
from jax import lax
from jax.experimental import pallas as pl
from jax.experimental.pallas import tpu as pltpu
from jax.sharding import PartitionSpec as P

F32 = jnp.float32
BF = jnp.bfloat16
MESH = pl.DeviceIdType.MESH

SIDE = 16
ATOMS = 384
GHOSTS = 256
SLOTS = 32
GROUP = 16
EDGES = GROUP * SLOTS
BLOCKS = ATOMS // GROUP
SHARES = ((0, 4), (4, 12), (12, 24))
EXT = ATOMS + 9 * GHOSTS
CUT = 6.25


def real_basis(count):
    n = np.arange(count)
    rows = np.zeros((count, count))
    slope = np.zeros((count, count))
    rows[0] = 1.0 / math.sqrt(count)
    rows[1] = np.where(n % 2 == 0, 1.0, -1.0) / math.sqrt(count)
    for k in range(1, count // 2):
        angle = 2.0 * math.pi * (k * n % count) / count
        rows[2 * k] = math.sqrt(2.0 / count) * np.cos(angle)
        rows[2 * k + 1] = math.sqrt(2.0 / count) * np.sin(angle)
        wave = 2.0 * math.pi * k / count
        slope[2 * k] = wave * rows[2 * k + 1]
        slope[2 * k + 1] = -wave * rows[2 * k]
    return rows, slope


def halves(table):
    high = table.astype(np.float32).astype(ml_dtypes.bfloat16)
    low = (table - high.astype(np.float64)).astype(np.float32).astype(ml_dtypes.bfloat16)
    return np.stack([high, low])


def grid_tables():
    basis, slope = real_basis(8 * SIDE)
    eye = np.eye(4)
    by = basis.reshape(SIDE, 2, 4, SIDE, 8)
    dy = slope.reshape(SIDE, 2, 4, SIDE, 8)
    y_forward = np.einsum("phkry,ab->hpkarby", by, eye).reshape(512, 512)
    y_back = np.stack(
        [
            np.einsum("phkry,ab->rayhpkb", by, eye),
            np.einsum("phkry,ab->rayhpkb", dy, eye),
        ]
    ).reshape(1024, 512)
    bx = basis.reshape(128, SIDE, 2, 4)
    dx = slope.reshape(128, SIDE, 2, 4)
    x_forward = np.einsum("sphx,ab->sapbhx", bx, eye)
    x_forward = x_forward.transpose(0, 1, 2, 4, 3, 5).reshape(512, 512)
    x_back = np.einsum("fsphx,ab->pfhbxsa", np.stack([bx, dx]), eye)
    x_back = x_back.reshape(1024, 512)
    z = np.arange(1024)
    coarse = 2.0 * math.pi * (32 * np.arange(16)[:, None] * z % 1024) / 1024
    fine = 2.0 * math.pi * (np.arange(32)[:, None] * z % 1024) / 1024
    scale = math.sqrt(2.0 / 1024)
    z_rows = np.concatenate(
        [np.cos(coarse), np.sin(coarse), scale * np.cos(fine), scale * np.sin(fine)]
    )
    return tuple(halves(t) for t in (y_forward, x_forward, x_back, y_back, z_rows))


def silu(x):
    half = 0.5 * x
    return half + half * jnp.tanh(half)


def transposed_left(a, b):
    return lax.dot_general(a, b, (((0,), (0,)), ((), ())), preferred_element_type=F32)


def transposed_right(a, b):
    return lax.dot_general(a, b, (((1,), (1,)), ((), ())), preferred_element_type=F32)


def fill_table(table, first, count, feat, pos, w_pair, shift_x, shift_y):
    flat = table.reshape(EXT * 8, 128)
    projected = jnp.dot(feat, w_pair, preferred_element_type=F32).astype(BF).astype(F32)
    lane = lax.broadcasted_iota(jnp.int32, (16, 384), 1)
    row = lax.broadcasted_iota(jnp.int32, (16, 384), 0)
    spread = (lane // 128 == row).astype(F32).astype(BF)
    xyz = transposed_left(pos, spread)
    parts = (
        projected[:, :128],
        projected[:, 128:],
        xyz[:, :128] + shift_x,
        xyz[:, 128:256] + shift_y,
        xyz[:, 256:],
    )
    for k, part in enumerate(parts):
        flat[pl.ds(first * 8 + k, count, stride=8), :] = part


def gather_edges(block, lists, table, picked, unroll):
    start = block * GROUP

    def one_slot(k, carry):
        for a in range(GROUP):
            j = lists[start + k * ATOMS + a]
            picked[k * GROUP + a] = table[j]
        return carry

    lax.fori_loop(0, SLOTS, one_slot, 0, unroll=unroll)


def edge_block(block, table, picked, own, radial_w, expand_w, contract_w, sums):
    first = pl.multiple_of(block * GROUP, GROUP)
    picked = picked.reshape(EDGES * 8, 128)
    table = table.reshape(EXT * 8, 128)

    def far(k):
        return picked[pl.ds(k, EDGES, stride=8), :].reshape(SLOTS, GROUP, 128)

    def near(k):
        return table[pl.ds(first * 8 + k, GROUP, stride=8), :][None]

    dx, dy, dz = far(2) - near(2), far(3) - near(3), far(4) - near(4)
    d2 = dx * dx + dy * dy + dz * dz
    lane = lax.broadcasted_iota(jnp.int32, (1, 1, 128), 2)
    u = d2 * (7.0 / CUT) - (lane % 8).astype(F32)
    basis = jnp.exp(-(u * u))
    envelope = jnp.square(jnp.maximum(0.0, 1.0 - d2 * (1.0 / CUT)))
    rest = basis - basis.astype(BF).astype(F32)
    left = jnp.where((lane >= 8) & (lane < 16), rest, basis).astype(BF)
    radial = jnp.dot(
        left.reshape(EDGES, 128), radial_w[...], preferred_element_type=F32
    ).reshape(SLOTS, GROUP, 128)
    edge_in = silu(radial + own[pl.ds(first, GROUP), :][None] + far(0))
    edge_in = edge_in.astype(BF).reshape(EDGES, 128)
    half = jnp.dot(edge_in, expand_w[...], preferred_element_type=F32)
    latent = (half + half * jnp.tanh(half)).astype(BF)
    mixed = jnp.dot(latent, contract_w[...], preferred_element_type=F32)
    weight = mixed.reshape(SLOTS, GROUP, 128) * envelope * far(1)
    scale = 1.0 / math.sqrt(SLOTS)
    for i, term in enumerate((weight, dx * weight, dy * weight, dz * weight)):
        sums[i, pl.ds(first, GROUP), :] = jnp.sum(term, axis=0) * scale


def edge_forces(sums, w_final):
    scalar, vx, vy, vz = (sums[i] for i in range(4))
    invariant = (scalar + (vx * vx + vy * vy + vz * vz) / 3.0).astype(BF)
    gate = silu(jnp.dot(invariant, w_final, preferred_element_type=F32))
    ones = jnp.ones((8, 128), F32)
    rows = [
        lax.dot_general(
            ones,
            v * gate,
            (((1,), (1,)), ((), ())),
            precision=lax.Precision.HIGHEST,
            preferred_element_type=F32,
        )[0:1]
        for v in (vx, vy, vz)
    ]
    return [row * (1.0 / math.sqrt(128.0)) for row in rows]


def two_halves(table, right):
    return jnp.dot(table[0], right, preferred_element_type=F32) + jnp.dot(
        table[1], right, preferred_element_type=F32
    )


def swap_halves(low, high):
    lane = lax.broadcasted_iota(jnp.int32, low.shape, low.ndim - 1)
    first = lane < 64
    turned_high = pltpu.roll(high, 64, high.ndim - 1)
    turned_low = pltpu.roll(low, 64, low.ndim - 1)
    return jnp.where(first, low, turned_high), jnp.where(first, turned_low, high)


def green_block(px, ry):
    row = lax.broadcasted_iota(jnp.int32, (512, 128), 0)
    lane = lax.broadcasted_iota(jnp.int32, (512, 128), 1)
    x_slot = row // 4
    y_slot = px * 8 + (lane // 64) * 4 + row % 4
    c = lane % 64
    x_mode = jnp.where(x_slot == 1, 64, x_slot // 2)
    y_mode = jnp.where(y_slot == 1, 64, y_slot // 2)
    z_mode = jnp.where((c == 32) & (ry == 0), 512, ry * 32 + c % 32)
    kx = x_mode.astype(F32) * (2.0 * math.pi / 128)
    ky = y_mode.astype(F32) * (2.0 * math.pi / 128)
    kz = z_mode.astype(F32) * (2.0 * math.pi / 1024)
    kk = kx * kx + ky * ky + kz * kz
    zero = (x_mode == 0) & (y_mode == 0) & (z_mode == 0)
    safe = jnp.where(zero, 1.0, kk)
    return jnp.where(zero, 0.0, 4.0 * math.pi * jnp.exp(-0.5 * kk) / safe)


class Exchange:
    def __init__(self, axis, outgoing, landing, sems):
        self.axis = axis
        self.outgoing, self.landing = outgoing, landing
        self.send_sem, self.recv_sem = sems.at[0], sems.at[1]
        self.me = lax.axis_index(axis)

    def copy(self, source, landing, target):
        return pltpu.make_async_remote_copy(
            src_ref=source,
            dst_ref=landing,
            send_sem=self.send_sem,
            recv_sem=self.recv_sem,
            device_id={self.axis: target},
            device_id_type=MESH,
        )

    def start(self):
        def one(step, carry):
            target = lax.rem(self.me + step, SIDE)
            self.copy(self.outgoing.at[target], self.landing.at[self.me], target).start()
            return carry

        lax.fori_loop(1, SIDE, one, 0, unroll=SIDE - 1)
        self.landing[self.me] = self.outgoing[self.me]

    def all_others(self):
        others = pl.ds(0, SIDE - 1)
        target = lax.rem(self.me + 1, SIDE)
        return self.copy(self.outgoing.at[others], self.landing.at[others], target)

    def wait_recv(self):
        self.all_others().wait_recv()

    def wait_send(self):
        self.all_others().wait_send()


GHOST_BLOCKS = (3, 5, 1, 7, 0, 2, 6, 8)


def device_kernel(
    count,
    feat,
    positions,
    exports,
    cells,
    w_self,
    w_pair,
    w_radial,
    w_final,
    w_charge,
    z_rows_far,
    w_expand_far,
    lists_far,
    y_forward_far,
    w_contract_far,
    x_forward_far,
    x_back_far,
    y_back_far,
    out,
    z_rows,
    w_expand,
    lists,
    y_forward,
    w_contract,
    x_forward,
    x_back,
    y_back,
    table,
    picked_even,
    picked_odd,
    own,
    radial_w,
    expand_w,
    sums,
    pos16,
    out_feat,
    out_pos,
    ghost_feat,
    ghost_pos,
    z_basis,
    send1,
    land1,
    send2,
    land2,
    send3,
    land3,
    send4,
    land4,
    green,
    sems,
    halo_sems,
    load_sems,
):
    px = lax.axis_index("dx")
    ry = lax.axis_index("dy")
    barrier = pltpu.get_barrier_semaphore()

    def greet(step, carry):
        pl.semaphore_signal(
            barrier,
            inc=1,
            device_id={"dx": lax.rem(px + step, SIDE), "dy": ry},
            device_id_type=MESH,
        )
        pl.semaphore_signal(
            barrier,
            inc=1,
            device_id={"dx": px, "dy": lax.rem(ry + step, SIDE)},
            device_id_type=MESH,
        )
        return carry

    lax.fori_loop(1, SIDE, greet, 0)
    for a in (1, SIDE - 1):
        for b in (1, SIDE - 1):
            pl.semaphore_signal(
                barrier,
                inc=1,
                device_id={"dx": lax.rem(px + a, SIDE), "dy": lax.rem(ry + b, SIDE)},
                device_id_type=MESH,
            )

    loads = [
        pltpu.make_async_copy(far, near, load_sems.at[i])
        for i, (far, near) in enumerate(
            (
                (z_rows_far, z_rows),
                (w_expand_far, w_expand),
                (y_forward_far, y_forward),
                (w_contract_far, w_contract),
                (x_forward_far, x_forward),
                (x_back_far, x_back),
                (y_back_far, y_back),
            )
            + ((lists_far, lists),)
        )
    ]
    for load in loads:
        load.start()

    pos16[...] = jnp.zeros_like(pos16)
    pos16[0:3, :] = positions[...].astype(F32)
    pos = pos16[...].astype(BF)
    slot = lax.broadcasted_iota(jnp.int32, (ATOMS, GHOSTS), 0)
    chosen = (slot == exports[...]).astype(F32).astype(BF)
    out_feat[...] = transposed_left(chosen, feat[...]).astype(BF)
    out_pos[...] = jnp.dot(pos, chosen, preferred_element_type=F32).astype(BF)

    cell = cells[...]
    height = cell % 1024
    column = cell // 1024
    level = lax.broadcasted_iota(jnp.int32, (1024, ATOMS), 0)
    at_height = (level == height).astype(F32).astype(BF)
    loads[0].wait()
    angles = two_halves(z_rows, at_height)
    fine_cos, fine_sin = angles[32:64], angles[64:96]
    root = math.sqrt(0.5)
    fine_row = lax.broadcasted_iota(jnp.int32, (32, ATOMS), 0)
    alternate = jnp.where(height % 2 == 0, 1.0, -1.0) * math.sqrt(1.0 / 1024)
    for r in range(SIDE):
        big_cos, big_sin = angles[r : r + 1], angles[16 + r : 17 + r]
        cosine = big_cos * fine_cos - big_sin * fine_sin
        sine = big_sin * fine_cos + big_cos * fine_sin
        if r == 0:
            cosine = jnp.where(fine_row == 0, cosine * root, cosine)
            sine = jnp.where(fine_row == 0, alternate, sine)
        z_basis[64 * r : 64 * r + 32, :] = cosine
        z_basis[64 * r + 32 : 64 * r + 64, :] = sine

    charge_w = jnp.broadcast_to(w_charge[...], (8, 128))
    atom = lax.broadcasted_iota(jnp.int32, (1, ATOMS), 1)
    live = atom < count[0, 0]
    charge = jnp.where(live, transposed_right(charge_w, feat[...])[0:1], 0.0)
    place = lax.broadcasted_iota(jnp.int32, (64, ATOMS), 0)
    at_column = (place == column).astype(F32).astype(BF)
    loaded = z_basis[...] * charge
    loaded_high = loaded.astype(BF)
    loaded_low = (loaded - loaded_high.astype(F32)).astype(BF)
    density = transposed_right(at_column, loaded_high) + transposed_right(at_column, loaded_low)
    for q in range(8):
        part = density[:, 128 * q : 128 * q + 128]
        even, odd = swap_halves(part[:32], part[32:])
        send1[2 * q] = even.astype(BF)
        send1[2 * q + 1] = odd.astype(BF)


    w_rad = w_radial[...]
    rad_high = w_rad.astype(BF).astype(F32)
    stacked = jnp.concatenate(
        [rad_high, rad_high, w_rad - rad_high, jnp.zeros((104, 128), F32)], axis=0
    )
    radial_w[...] = stacked.astype(BF)
    loads[1].wait()
    expand_w[...] = (w_expand[...].astype(F32) * 0.5).astype(BF)
    own[...] = jnp.dot(feat[...], w_self[...], preferred_element_type=F32)
    fill_table(table, 0, ATOMS, feat[...], pos, w_pair[...], 0.0, 0.0)
    green[...] = green_block(px, ry)

    pl.semaphore_wait(barrier, 34)
    over_y = Exchange("dy", send1, land1, sems.at[0])
    over_x = Exchange("dx", send2, land2, sems.at[1])
    back_x = Exchange("dx", send3, land3, sems.at[2])
    back_y = Exchange("dy", send4, land4, sems.at[3])
    over_y.start()
    halo = {}
    for i, b in enumerate(GHOST_BLOCKS):
        target = {
            "dx": lax.rem(px + SIDE + 1 - b // 3, SIDE),
            "dy": lax.rem(ry + SIDE + 1 - b % 3, SIDE),
        }
        for j, (source, landing) in enumerate(((out_feat, ghost_feat), (out_pos, ghost_pos))):
            copy = pltpu.make_async_remote_copy(
                src_ref=source,
                dst_ref=landing.at[b],
                send_sem=halo_sems.at[j, i],
                recv_sem=halo_sems.at[2 + j, i],
                device_id=target,
                device_id_type=MESH,
            )
            copy.start()
            halo[b, j] = copy

    over_y.wait_recv()
    loads[2].wait()
    along_y = two_halves(y_forward, land1[...].reshape(512, 128))
    low, high = swap_halves(along_y[:256], along_y[256:])
    send2[:, 0:16, :] = low.astype(BF).reshape(SIDE, 16, 128)
    send2[:, 16:32, :] = high.astype(BF).reshape(SIDE, 16, 128)
    over_x.start()

    for b in GHOST_BLOCKS:
        halo[b, 0].wait_recv()
        halo[b, 1].wait_recv()
        fill_table(
            table,
            ATOMS + GHOSTS * b,
            GHOSTS,
            ghost_feat[b],
            ghost_pos[b],
            w_pair[...],
            b // 3 - 1.0,
            b % 3 - 1.0,
        )

    def edges(start, stop):
        fixed = (own, radial_w, expand_w, w_contract, sums)

        def pair(h, carry):
            block = 2 * h
            gather_edges(block + 1, lists, table, picked_odd, SLOTS)
            edge_block(block, table, picked_even, *fixed)
            following = jnp.minimum(block + 2, BLOCKS - 1)
            gather_edges(following, lists, table, picked_even, SLOTS)
            edge_block(block + 1, table, picked_odd, *fixed)
            return carry

        lax.fori_loop(start // 2, stop // 2, pair, 0)

    for i in (3, 7):
        loads[i].wait()
    gather_edges(0, lists, table, picked_even, 1)
    edges(*SHARES[0])

    over_x.wait_recv()
    loads[4].wait()
    loads[5].wait()
    spectrum = two_halves(x_forward, land2[...].reshape(512, 128)) * green[...]
    top = spectrum.astype(BF)
    rest = (spectrum - top.astype(F32)).astype(BF)
    along_x = two_halves(x_back, top) + jnp.dot(x_back[0], rest, preferred_element_type=F32)
    send3[...] = along_x.astype(BF).reshape(SIDE, 64, 128)
    back_x.start()
    edges(*SHARES[1])

    back_x.wait_recv()
    loads[6].wait()
    arrived = []
    for f in range(2):
        low = land3[:, 32 * f : 32 * f + 16, :].astype(F32).reshape(256, 128)
        high = land3[:, 32 * f + 16 : 32 * f + 32, :].astype(F32).reshape(256, 128)
        low, high = swap_halves(low, high)
        arrived.append(jnp.concatenate([low, high], axis=0).astype(BF))
    from_potential = two_halves(y_back, arrived[0]).astype(BF).reshape(2, SIDE, 32, 128)
    from_slope = (
        jnp.dot(y_back[0, 0:512], arrived[1], preferred_element_type=F32)
        + jnp.dot(y_back[1, 0:512], arrived[1], preferred_element_type=F32)
    )
    send4[:, 0:32, :] = from_potential[0]
    send4[:, 32:64, :] = from_slope.astype(BF).reshape(SIDE, 32, 128)
    send4[:, 64:96, :] = from_potential[1]
    back_y.start()
    edges(*SHARES[2])
    short = edge_forces(sums, w_final[...])

    back_y.wait_recv()
    fields = []
    for f in range(3):
        lows, highs = [], []
        for q in range(8):
            low, high = swap_halves(
                land4[2 * q, 32 * f : 32 * f + 32, :].astype(F32),
                land4[2 * q + 1, 32 * f : 32 * f + 32, :].astype(F32),
            )
            lows.append(low)
            highs.append(high)
        coefficients = jnp.concatenate(
            [jnp.concatenate(lows, axis=1), jnp.concatenate(highs, axis=1)], axis=0
        ).astype(BF)
        fields.append(transposed_left(coefficients, at_column))
    potential, slope_x, slope_y = fields
    values = z_basis[...]
    field_x = jnp.sum(slope_x * values, axis=0, keepdims=True)
    field_y = jnp.sum(slope_y * values, axis=0, keepdims=True)
    pairs = potential.reshape(SIDE, 64, ATOMS)
    basis = values.reshape(SIDE, 64, ATOMS)
    wave = (
        lax.broadcasted_iota(jnp.int32, (SIDE, 32, ATOMS), 0) * 32
        + lax.broadcasted_iota(jnp.int32, (SIDE, 32, ATOMS), 1)
    ).astype(F32) * (2.0 * math.pi / 1024)
    turned = wave * (pairs[:, :32] * basis[:, 32:] - pairs[:, 32:] * basis[:, :32])
    field_z = jnp.sum(turned.reshape(512, ATOMS), axis=0, keepdims=True)
    for a, field in enumerate((field_x, field_y, field_z)):
        out[a : a + 1, :] = jnp.where(live, short[a] + charge * field, 0.0)

    for copy in halo.values():
        copy.wait_send()
    for exchange in (over_y, over_x, back_x, back_y):
        exchange.wait_send()


def shards(
    features,
    positions,
    atom_count,
    ghost_index,
    neighbour_list,
    cell_index,
    w_self,
    w_pair,
    w_radial,
    w_expand,
    w_contract,
    w_final,
    w_charge,
):
    y_forward, x_forward, x_back, y_back, z_rows = (jnp.asarray(t) for t in grid_tables())
    vmem = pl.BlockSpec(memory_space=pltpu.VMEM)
    smem = pl.BlockSpec(memory_space=pltpu.SMEM)
    far = pl.BlockSpec(memory_space=pl.ANY)
    forces = pl.pallas_call(
        device_kernel,
        out_shape=jax.ShapeDtypeStruct((3, ATOMS), F32),
        in_specs=[smem] + [vmem] * 9 + [far] * 8,
        out_specs=vmem,
        scratch_shapes=[
            pltpu.VMEM((2, 96, 1024), BF),
            pltpu.VMEM((128, 1024), BF),
            pltpu.SMEM((SLOTS * ATOMS,), jnp.int32),
            pltpu.VMEM((2, 512, 512), BF),
            pltpu.VMEM((1024, 128), BF),
            pltpu.VMEM((2, 512, 512), BF),
            pltpu.VMEM((2, 1024, 512), BF),
            pltpu.VMEM((2, 1024, 512), BF),
            pltpu.VMEM((EXT, 8, 128), F32),
            pltpu.VMEM((EDGES, 8, 128), F32),
            pltpu.VMEM((EDGES, 8, 128), F32),
            pltpu.VMEM((ATOMS, 128), F32),
            pltpu.VMEM((128, 128), BF),
            pltpu.VMEM((128, 1024), BF),
            pltpu.VMEM((4, ATOMS, 128), F32),
            pltpu.VMEM((16, ATOMS), F32),
            pltpu.VMEM((GHOSTS, 128), BF),
            pltpu.VMEM((16, GHOSTS), BF),
            pltpu.VMEM((9, GHOSTS, 128), BF),
            pltpu.VMEM((9, 16, GHOSTS), BF),
            pltpu.VMEM((1024, ATOMS), F32),
            pltpu.VMEM((SIDE, 32, 128), BF),
            pltpu.VMEM((SIDE, 32, 128), BF),
            pltpu.VMEM((SIDE, 32, 128), BF),
            pltpu.VMEM((SIDE, 32, 128), BF),
            pltpu.VMEM((SIDE, 64, 128), BF),
            pltpu.VMEM((SIDE, 64, 128), BF),
            pltpu.VMEM((SIDE, 96, 128), BF),
            pltpu.VMEM((SIDE, 96, 128), BF),
            pltpu.VMEM((512, 128), F32),
            pltpu.SemaphoreType.DMA((4, 2)),
            pltpu.SemaphoreType.DMA((4, 8)),
            pltpu.SemaphoreType.DMA((8,)),
        ],
        compiler_params=pltpu.CompilerParams(
            collective_id=0, has_side_effects=True, vmem_limit_bytes=58 * 2**20
        ),
        name="forces",
    )(
        atom_count,
        features[0, 0],
        positions[0, 0],
        ghost_index[0],
        cell_index[0],
        w_self,
        w_pair,
        w_radial,
        w_final,
        w_charge[None],
        z_rows,
        w_expand,
        neighbour_list[0, 0].T.reshape(-1),
        y_forward,
        w_contract,
        x_forward,
        x_back,
        y_back,
    )
    return forces[None, None]


def solution(mesh):
    whole = P()
    placed = (
        P("dx", "dy", None, None),
        P("dx", "dy", None, None),
        P("dx", "dy"),
        P("dx", "dy", None),
        P("dx", "dy", None, None),
        P("dx", "dy", None),
    ) + (whole,) * 7
    return jax.shard_map(
        shards, mesh=mesh, in_specs=placed, out_specs=P("dx", "dy", None, None), check_vma=False
    )
```

```python
import functools
import math

import numpy as np
import ml_dtypes

import jax
import jax.numpy as jnp
from jax import lax
from jax.experimental import pallas as pl
from jax.experimental.pallas import tpu as pltpu
from jax.sharding import PartitionSpec as P

F32 = jnp.float32
BF = jnp.bfloat16
MESH = pl.DeviceIdType.MESH

SIDE = 16
ATOMS = 384
GHOSTS = 256
SLOTS = 32
GROUP = 16
EDGES = GROUP * SLOTS
BLOCKS = ATOMS // GROUP
PIECE = 256
SHARES = ((0, 6), (6, 14), (14, 24))
EXT = ATOMS + 9 * GHOSTS
CUT = 6.25


def real_basis(count):
    n = np.arange(count)
    rows = np.zeros((count, count))
    slope = np.zeros((count, count))
    rows[0] = 1.0 / math.sqrt(count)
    rows[1] = np.where(n % 2 == 0, 1.0, -1.0) / math.sqrt(count)
    for k in range(1, count // 2):
        angle = 2.0 * math.pi * (k * n % count) / count
        rows[2 * k] = math.sqrt(2.0 / count) * np.cos(angle)
        rows[2 * k + 1] = math.sqrt(2.0 / count) * np.sin(angle)
        wave = 2.0 * math.pi * k / count
        slope[2 * k] = wave * rows[2 * k + 1]
        slope[2 * k + 1] = -wave * rows[2 * k]
    return rows, slope


def halves(table):
    high = table.astype(np.float32).astype(ml_dtypes.bfloat16)
    low = (table - high.astype(np.float64)).astype(np.float32).astype(ml_dtypes.bfloat16)
    return np.stack([high, low])


def grid_tables():
    basis, slope = real_basis(8 * SIDE)
    eye = np.eye(4)
    by = basis.reshape(SIDE, 2, 4, SIDE, 8)
    dy = slope.reshape(SIDE, 2, 4, SIDE, 8)
    y_forward = np.einsum("phkry,ab->hpkarby", by, eye).reshape(512, 512)
    y_back = np.stack(
        [
            np.einsum("phkry,ab->rayhpkb", by, eye),
            np.einsum("phkry,ab->rayhpkb", dy, eye),
        ]
    ).reshape(1024, 512)
    bx = basis.reshape(128, SIDE, 2, 4)
    dx = slope.reshape(128, SIDE, 2, 4)
    x_forward = np.einsum("sphx,ab->sapbhx", bx, eye)
    x_forward = x_forward.transpose(0, 1, 2, 4, 3, 5).reshape(512, 512)
    x_back = np.einsum("fsphx,ab->pfhbxsa", np.stack([bx, dx]), eye)
    x_back = x_back.reshape(1024, 512)
    z = np.arange(1024)
    coarse = 2.0 * math.pi * (32 * np.arange(16)[:, None] * z % 1024) / 1024
    fine = 2.0 * math.pi * (np.arange(32)[:, None] * z % 1024) / 1024
    scale = math.sqrt(2.0 / 1024)
    z_rows = np.concatenate(
        [np.cos(coarse), np.sin(coarse), scale * np.cos(fine), scale * np.sin(fine)]
    )
    return tuple(halves(t) for t in (y_forward, x_forward, x_back, y_back, z_rows))


def silu(x):
    half = 0.5 * x
    return half + half * jnp.tanh(half)


def transposed_left(a, b):
    return lax.dot_general(a, b, (((0,), (0,)), ((), ())), preferred_element_type=F32)


def transposed_right(a, b):
    return lax.dot_general(a, b, (((1,), (1,)), ((), ())), preferred_element_type=F32)


def fill_table(table, first, count, feat, pos, w_pair, shift_x, shift_y):
    flat = table.reshape(EXT * 8, 128)
    projected = jnp.dot(feat, w_pair, preferred_element_type=F32).astype(BF).astype(F32)
    lane = lax.broadcasted_iota(jnp.int32, (16, 384), 1)
    row = lax.broadcasted_iota(jnp.int32, (16, 384), 0)
    spread = (lane // 128 == row).astype(F32).astype(BF)
    xyz = transposed_left(pos, spread)
    parts = (
        projected[:, :128],
        projected[:, 128:],
        xyz[:, :128] + shift_x,
        xyz[:, 128:256] + shift_y,
        xyz[:, 256:],
    )
    for k, part in enumerate(parts):
        flat[pl.ds(first * 8 + k, count, stride=8), :] = part


def gather_edges(block, first, count, lists, table, picked, unroll):
    start = block * GROUP

    def one_slot(i, carry):
        k = first + i
        for a in range(GROUP):
            j = lists[start + k * ATOMS + a]
            picked[k * GROUP + a] = table[j]
        return carry

    lax.fori_loop(0, count, one_slot, 0, unroll=unroll)


def edge_inputs(block, slot, count, table, picked, own, radial_w, hidden, gains):
    first = pl.multiple_of(block * GROUP, GROUP)
    rows = count * GROUP
    picked = picked.reshape(EDGES * 8, 128)
    table = table.reshape(EXT * 8, 128)

    def far(k):
        start = slot * GROUP * 8 + k
        return picked[pl.ds(start, rows, stride=8), :].reshape(count, GROUP, 128)

    def near(k):
        return table[pl.ds(first * 8 + k, GROUP, stride=8), :][None]

    dx, dy, dz = far(2) - near(2), far(3) - near(3), far(4) - near(4)
    d2 = dx * dx + dy * dy + dz * dz
    lane = lax.broadcasted_iota(jnp.int32, (1, 1, 128), 2)
    u = d2 * (7.0 / CUT) - (lane % 8).astype(F32)
    basis = jnp.exp(-(u * u))
    envelope = jnp.square(jnp.maximum(0.0, 1.0 - d2 * (1.0 / CUT)))
    rest = basis - basis.astype(BF).astype(F32)
    left = jnp.where((lane >= 8) & (lane < 16), rest, basis).astype(BF)
    radial = jnp.dot(
        left.reshape(rows, 128), radial_w[...], preferred_element_type=F32
    ).reshape(count, GROUP, 128)
    edge_in = silu(radial + own[pl.ds(first, GROUP), :][None] + far(0))
    hidden[slot * GROUP : slot * GROUP + rows] = edge_in.astype(BF).reshape(rows, 128)
    gain = envelope * far(1)
    for i, term in enumerate((gain, dx * gain, dy * gain, dz * gain)):
        gains[i, slot : slot + count] = term


def edge_step(block, lists, table, picked, hidden, gains, own, radial_w, expand_w, contract_w, sums):
    last = BLOCKS - 1
    totals = None
    for m in range(0, EDGES, PIECE):
        slot, count = m // GROUP, PIECE // GROUP
        gather_edges(jnp.minimum(block + 2, last), slot, count, lists, table, picked[0], count)
        following = jnp.minimum(block + 1, last)
        edge_inputs(
            following, slot, count, table, picked[1], own, radial_w, hidden[1], gains[1]
        )
        half = jnp.dot(hidden[0][m : m + PIECE], expand_w[...], preferred_element_type=F32)
        latent = (half + half * jnp.tanh(half)).astype(BF)
        mixed = jnp.dot(latent, contract_w[...], preferred_element_type=F32)
        mixed = mixed.reshape(count, GROUP, 128)
        part = [jnp.sum(mixed * gains[0][i, slot : slot + count], axis=0) for i in range(4)]
        totals = part if totals is None else [x + y for x, y in zip(totals, part)]
    first = pl.multiple_of(block * GROUP, GROUP)
    for i in range(4):
        sums[i, pl.ds(first, GROUP), :] = totals[i] * (1.0 / math.sqrt(SLOTS))


def edge_forces(sums, w_final):
    scalar, vx, vy, vz = (sums[i] for i in range(4))
    invariant = (scalar + (vx * vx + vy * vy + vz * vz) / 3.0).astype(BF)
    gate = silu(jnp.dot(invariant, w_final, preferred_element_type=F32))
    ones = jnp.ones((8, 128), F32)
    rows = [
        lax.dot_general(
            ones,
            v * gate,
            (((1,), (1,)), ((), ())),
            precision=lax.Precision.HIGHEST,
            preferred_element_type=F32,
        )[0:1]
        for v in (vx, vy, vz)
    ]
    return [row * (1.0 / math.sqrt(128.0)) for row in rows]


def two_halves(table, right):
    return jnp.dot(table[0], right, preferred_element_type=F32) + jnp.dot(
        table[1], right, preferred_element_type=F32
    )


def swap_halves(low, high):
    lane = lax.broadcasted_iota(jnp.int32, low.shape, low.ndim - 1)
    first = lane < 64
    turned_high = pltpu.roll(high, 64, high.ndim - 1)
    turned_low = pltpu.roll(low, 64, low.ndim - 1)
    return jnp.where(first, low, turned_high), jnp.where(first, turned_low, high)


def green_block(px, ry):
    row = lax.broadcasted_iota(jnp.int32, (512, 128), 0)
    lane = lax.broadcasted_iota(jnp.int32, (512, 128), 1)
    x_slot = row // 4
    y_slot = px * 8 + (lane // 64) * 4 + row % 4
    c = lane % 64
    x_mode = jnp.where(x_slot == 1, 64, x_slot // 2)
    y_mode = jnp.where(y_slot == 1, 64, y_slot // 2)
    z_mode = jnp.where((c == 32) & (ry == 0), 512, ry * 32 + c % 32)
    kx = x_mode.astype(F32) * (2.0 * math.pi / 128)
    ky = y_mode.astype(F32) * (2.0 * math.pi / 128)
    kz = z_mode.astype(F32) * (2.0 * math.pi / 1024)
    kk = kx * kx + ky * ky + kz * kz
    zero = (x_mode == 0) & (y_mode == 0) & (z_mode == 0)
    safe = jnp.where(zero, 1.0, kk)
    return jnp.where(zero, 0.0, 4.0 * math.pi * jnp.exp(-0.5 * kk) / safe)


class Exchange:
    def __init__(self, axis, outgoing, landing, sems):
        self.axis = axis
        self.outgoing, self.landing = outgoing, landing
        self.send_sem, self.recv_sem = sems.at[0], sems.at[1]
        self.me = lax.axis_index(axis)

    def copy(self, source, landing, target):
        return pltpu.make_async_remote_copy(
            src_ref=source,
            dst_ref=landing,
            send_sem=self.send_sem,
            recv_sem=self.recv_sem,
            device_id={self.axis: target},
            device_id_type=MESH,
        )

    def start(self):
        def one(step, carry):
            target = lax.rem(self.me + step, SIDE)
            self.copy(self.outgoing.at[target], self.landing.at[self.me], target).start()
            return carry

        lax.fori_loop(1, SIDE, one, 0, unroll=SIDE - 1)
        self.landing[self.me] = self.outgoing[self.me]

    def all_others(self):
        others = pl.ds(0, SIDE - 1)
        target = lax.rem(self.me + 1, SIDE)
        return self.copy(self.outgoing.at[others], self.landing.at[others], target)

    def wait_recv(self):
        self.all_others().wait_recv()

    def wait_send(self):
        self.all_others().wait_send()


GHOST_BLOCKS = (3, 5, 1, 7, 0, 2, 6, 8)


def device_kernel(
    count,
    feat,
    positions,
    exports,
    cells,
    w_self,
    w_pair,
    w_radial,
    w_final,
    w_charge,
    z_rows_far,
    w_expand_far,
    lists_far,
    y_forward_far,
    w_contract_far,
    x_forward_far,
    x_back_far,
    y_back_far,
    out,
    z_rows,
    w_expand,
    lists,
    y_forward,
    w_contract,
    x_forward,
    x_back,
    y_back,
    table,
    picked_even,
    picked_odd,
    hidden_even,
    hidden_odd,
    gains_even,
    gains_odd,
    own,
    radial_w,
    expand_w,
    sums,
    pos16,
    out_feat,
    out_pos,
    ghost_feat,
    ghost_pos,
    z_basis,
    send1,
    land1,
    send2,
    land2,
    send3,
    land3,
    send4,
    land4,
    green,
    sems,
    halo_sems,
    load_sems,
):
    px = lax.axis_index("dx")
    ry = lax.axis_index("dy")
    barrier = pltpu.get_barrier_semaphore()

    def greet(step, carry):
        pl.semaphore_signal(
            barrier,
            inc=1,
            device_id={"dx": lax.rem(px + step, SIDE), "dy": ry},
            device_id_type=MESH,
        )
        pl.semaphore_signal(
            barrier,
            inc=1,
            device_id={"dx": px, "dy": lax.rem(ry + step, SIDE)},
            device_id_type=MESH,
        )
        return carry

    lax.fori_loop(1, SIDE, greet, 0)
    for a in (1, SIDE - 1):
        for b in (1, SIDE - 1):
            pl.semaphore_signal(
                barrier,
                inc=1,
                device_id={"dx": lax.rem(px + a, SIDE), "dy": lax.rem(ry + b, SIDE)},
                device_id_type=MESH,
            )

    loads = [
        pltpu.make_async_copy(far, near, load_sems.at[i])
        for i, (far, near) in enumerate(
            (
                (z_rows_far, z_rows),
                (w_expand_far, w_expand),
                (y_forward_far, y_forward),
                (w_contract_far, w_contract),
                (x_forward_far, x_forward),
                (x_back_far, x_back),
                (y_back_far, y_back),
            )
            + ((lists_far, lists),)
        )
    ]
    for load in loads:
        load.start()

    pos16[...] = jnp.zeros_like(pos16)
    pos16[0:3, :] = positions[...].astype(F32)
    pos = pos16[...].astype(BF)
    slot = lax.broadcasted_iota(jnp.int32, (ATOMS, GHOSTS), 0)
    chosen = (slot == exports[...]).astype(F32).astype(BF)
    out_feat[...] = transposed_left(chosen, feat[...]).astype(BF)
    out_pos[...] = jnp.dot(pos, chosen, preferred_element_type=F32).astype(BF)

    cell = cells[...]
    height = cell % 1024
    column = cell // 1024
    level = lax.broadcasted_iota(jnp.int32, (1024, ATOMS), 0)
    at_height = (level == height).astype(F32).astype(BF)
    loads[0].wait()
    angles = two_halves(z_rows, at_height)
    fine_cos, fine_sin = angles[32:64], angles[64:96]
    root = math.sqrt(0.5)
    fine_row = lax.broadcasted_iota(jnp.int32, (32, ATOMS), 0)
    alternate = jnp.where(height % 2 == 0, 1.0, -1.0) * math.sqrt(1.0 / 1024)
    for r in range(SIDE):
        big_cos, big_sin = angles[r : r + 1], angles[16 + r : 17 + r]
        cosine = big_cos * fine_cos - big_sin * fine_sin
        sine = big_sin * fine_cos + big_cos * fine_sin
        if r == 0:
            cosine = jnp.where(fine_row == 0, cosine * root, cosine)
            sine = jnp.where(fine_row == 0, alternate, sine)
        z_basis[64 * r : 64 * r + 32, :] = cosine
        z_basis[64 * r + 32 : 64 * r + 64, :] = sine

    charge_w = jnp.broadcast_to(w_charge[...], (8, 128))
    atom = lax.broadcasted_iota(jnp.int32, (1, ATOMS), 1)
    live = atom < count[0, 0]
    charge = jnp.where(live, transposed_right(charge_w, feat[...])[0:1], 0.0)
    place = lax.broadcasted_iota(jnp.int32, (64, ATOMS), 0)
    at_column = (place == column).astype(F32).astype(BF)
    loaded = z_basis[...] * charge
    loaded_high = loaded.astype(BF)
    loaded_low = (loaded - loaded_high.astype(F32)).astype(BF)
    density = transposed_right(at_column, loaded_high) + transposed_right(at_column, loaded_low)
    for q in range(8):
        part = density[:, 128 * q : 128 * q + 128]
        even, odd = swap_halves(part[:32], part[32:])
        send1[2 * q] = even.astype(BF)
        send1[2 * q + 1] = odd.astype(BF)


    w_rad = w_radial[...]
    rad_high = w_rad.astype(BF).astype(F32)
    stacked = jnp.concatenate(
        [rad_high, rad_high, w_rad - rad_high, jnp.zeros((104, 128), F32)], axis=0
    )
    radial_w[...] = stacked.astype(BF)
    loads[1].wait()
    expand_w[...] = (w_expand[...].astype(F32) * 0.5).astype(BF)
    own[...] = jnp.dot(feat[...], w_self[...], preferred_element_type=F32)
    fill_table(table, 0, ATOMS, feat[...], pos, w_pair[...], 0.0, 0.0)
    green[...] = green_block(px, ry)

    pl.semaphore_wait(barrier, 34)
    over_y = Exchange("dy", send1, land1, sems.at[0])
    over_x = Exchange("dx", send2, land2, sems.at[1])
    back_x = Exchange("dx", send3, land3, sems.at[2])
    back_y = Exchange("dy", send4, land4, sems.at[3])
    halo = {}
    for i, b in enumerate(GHOST_BLOCKS):
        target = {
            "dx": lax.rem(px + SIDE + 1 - b // 3, SIDE),
            "dy": lax.rem(ry + SIDE + 1 - b % 3, SIDE),
        }
        for j, (source, landing) in enumerate(((out_feat, ghost_feat), (out_pos, ghost_pos))):
            copy = pltpu.make_async_remote_copy(
                src_ref=source,
                dst_ref=landing.at[b],
                send_sem=halo_sems.at[j, i],
                recv_sem=halo_sems.at[2 + j, i],
                device_id=target,
                device_id_type=MESH,
            )
            copy.start()
            halo[b, j] = copy
    over_y.start()

    over_y.wait_recv()
    loads[2].wait()
    along_y = two_halves(y_forward, land1[...].reshape(512, 128))
    low, high = swap_halves(along_y[:256], along_y[256:])
    send2[:, 0:16, :] = low.astype(BF).reshape(SIDE, 16, 128)
    send2[:, 16:32, :] = high.astype(BF).reshape(SIDE, 16, 128)
    over_x.start()

    for b in GHOST_BLOCKS:
        halo[b, 0].wait_recv()
        halo[b, 1].wait_recv()
        fill_table(
            table,
            ATOMS + GHOSTS * b,
            GHOSTS,
            ghost_feat[b],
            ghost_pos[b],
            w_pair[...],
            b // 3 - 1.0,
            b % 3 - 1.0,
        )

    def edges(start, stop):
        fixed = (own, radial_w, expand_w, w_contract, sums)
        even = (picked_even, picked_odd), (hidden_even, hidden_odd), (gains_even, gains_odd)
        odd = tuple(pair[::-1] for pair in even)

        def pair(h, carry):
            edge_step(2 * h, lists, table, *even, *fixed)
            edge_step(2 * h + 1, lists, table, *odd, *fixed)
            return carry

        lax.fori_loop(start // 2, stop // 2, pair, 0)

    for i in (3, 7):
        loads[i].wait()
    gather_edges(0, 0, SLOTS, lists, table, picked_even, 2)
    gather_edges(1, 0, SLOTS, lists, table, picked_odd, 2)
    edge_inputs(0, 0, SLOTS, table, picked_even, own, radial_w, hidden_even, gains_even)
    edges(*SHARES[0])

    over_x.wait_recv()
    loads[4].wait()
    loads[5].wait()
    spectrum = two_halves(x_forward, land2[...].reshape(512, 128)) * green[...]
    top = spectrum.astype(BF)
    rest = (spectrum - top.astype(F32)).astype(BF)
    along_x = two_halves(x_back, top) + jnp.dot(x_back[0], rest, preferred_element_type=F32)
    send3[...] = along_x.astype(BF).reshape(SIDE, 64, 128)
    back_x.start()
    edges(*SHARES[1])

    back_x.wait_recv()
    loads[6].wait()
    arrived = []
    for f in range(2):
        low = land3[:, 32 * f : 32 * f + 16, :].astype(F32).reshape(256, 128)
        high = land3[:, 32 * f + 16 : 32 * f + 32, :].astype(F32).reshape(256, 128)
        low, high = swap_halves(low, high)
        arrived.append(jnp.concatenate([low, high], axis=0).astype(BF))
    from_potential = two_halves(y_back, arrived[0]).astype(BF).reshape(2, SIDE, 32, 128)
    from_slope = (
        jnp.dot(y_back[0, 0:512], arrived[1], preferred_element_type=F32)
        + jnp.dot(y_back[1, 0:512], arrived[1], preferred_element_type=F32)
    )
    send4[:, 0:32, :] = from_potential[0]
    send4[:, 32:64, :] = from_slope.astype(BF).reshape(SIDE, 32, 128)
    send4[:, 64:96, :] = from_potential[1]
    back_y.start()
    edges(*SHARES[2])
    short = edge_forces(sums, w_final[...])

    back_y.wait_recv()
    fields = []
    for f in range(3):
        lows, highs = [], []
        for q in range(8):
            low, high = swap_halves(
                land4[2 * q, 32 * f : 32 * f + 32, :].astype(F32),
                land4[2 * q + 1, 32 * f : 32 * f + 32, :].astype(F32),
            )
            lows.append(low)
            highs.append(high)
        coefficients = jnp.concatenate(
            [jnp.concatenate(lows, axis=1), jnp.concatenate(highs, axis=1)], axis=0
        ).astype(BF)
        fields.append(transposed_left(coefficients, at_column))
    potential, slope_x, slope_y = fields
    values = z_basis[...]
    field_x = jnp.sum(slope_x * values, axis=0, keepdims=True)
    field_y = jnp.sum(slope_y * values, axis=0, keepdims=True)
    pairs = potential.reshape(SIDE, 64, ATOMS)
    basis = values.reshape(SIDE, 64, ATOMS)
    wave = (
        lax.broadcasted_iota(jnp.int32, (SIDE, 32, ATOMS), 0) * 32
        + lax.broadcasted_iota(jnp.int32, (SIDE, 32, ATOMS), 1)
    ).astype(F32) * (2.0 * math.pi / 1024)
    turned = wave * (pairs[:, :32] * basis[:, 32:] - pairs[:, 32:] * basis[:, :32])
    field_z = jnp.sum(turned.reshape(512, ATOMS), axis=0, keepdims=True)
    for a, field in enumerate((field_x, field_y, field_z)):
        out[a : a + 1, :] = jnp.where(live, short[a] + charge * field, 0.0)

    for copy in halo.values():
        copy.wait_send()
    for exchange in (over_y, over_x, back_x, back_y):
        exchange.wait_send()


def shards(
    features,
    positions,
    atom_count,
    ghost_index,
    neighbour_list,
    cell_index,
    w_self,
    w_pair,
    w_radial,
    w_expand,
    w_contract,
    w_final,
    w_charge,
):
    y_forward, x_forward, x_back, y_back, z_rows = (jnp.asarray(t) for t in grid_tables())
    vmem = pl.BlockSpec(memory_space=pltpu.VMEM)
    smem = pl.BlockSpec(memory_space=pltpu.SMEM)
    far = pl.BlockSpec(memory_space=pl.ANY)
    forces = pl.pallas_call(
        device_kernel,
        out_shape=jax.ShapeDtypeStruct((3, ATOMS), F32),
        in_specs=[smem] + [vmem] * 9 + [far] * 8,
        out_specs=vmem,
        scratch_shapes=[
            pltpu.VMEM((2, 96, 1024), BF),
            pltpu.VMEM((128, 1024), BF),
            pltpu.SMEM((SLOTS * ATOMS,), jnp.int32),
            pltpu.VMEM((2, 512, 512), BF),
            pltpu.VMEM((1024, 128), BF),
            pltpu.VMEM((2, 512, 512), BF),
            pltpu.VMEM((2, 1024, 512), BF),
            pltpu.VMEM((2, 1024, 512), BF),
            pltpu.VMEM((EXT, 8, 128), F32),
            pltpu.VMEM((EDGES, 8, 128), F32),
            pltpu.VMEM((EDGES, 8, 128), F32),
            pltpu.VMEM((EDGES, 128), BF),
            pltpu.VMEM((EDGES, 128), BF),
            pltpu.VMEM((4, SLOTS, GROUP, 128), F32),
            pltpu.VMEM((4, SLOTS, GROUP, 128), F32),
            pltpu.VMEM((ATOMS, 128), F32),
            pltpu.VMEM((128, 128), BF),
            pltpu.VMEM((128, 1024), BF),
            pltpu.VMEM((4, ATOMS, 128), F32),
            pltpu.VMEM((16, ATOMS), F32),
            pltpu.VMEM((GHOSTS, 128), BF),
            pltpu.VMEM((16, GHOSTS), BF),
            pltpu.VMEM((9, GHOSTS, 128), BF),
            pltpu.VMEM((9, 16, GHOSTS), BF),
            pltpu.VMEM((1024, ATOMS), F32),
            pltpu.VMEM((SIDE, 32, 128), BF),
            pltpu.VMEM((SIDE, 32, 128), BF),
            pltpu.VMEM((SIDE, 32, 128), BF),
            pltpu.VMEM((SIDE, 32, 128), BF),
            pltpu.VMEM((SIDE, 64, 128), BF),
            pltpu.VMEM((SIDE, 64, 128), BF),
            pltpu.VMEM((SIDE, 96, 128), BF),
            pltpu.VMEM((SIDE, 96, 128), BF),
            pltpu.VMEM((512, 128), F32),
            pltpu.SemaphoreType.DMA((4, 2)),
            pltpu.SemaphoreType.DMA((4, 8)),
            pltpu.SemaphoreType.DMA((8,)),
        ],
        compiler_params=pltpu.CompilerParams(
            collective_id=0, has_side_effects=True, vmem_limit_bytes=58 * 2**20
        ),
        name="forces",
    )(
        atom_count,
        features[0, 0],
        positions[0, 0],
        ghost_index[0],
        cell_index[0],
        w_self,
        w_pair,
        w_radial,
        w_final,
        w_charge[None],
        z_rows,
        w_expand,
        neighbour_list[0, 0].T.reshape(-1),
        y_forward,
        w_contract,
        x_forward,
        x_back,
        y_back,
    )
    return forces[None, None]


def solution(mesh):
    whole = P()
    placed = (
        P("dx", "dy", None, None),
        P("dx", "dy", None, None),
        P("dx", "dy"),
        P("dx", "dy", None),
        P("dx", "dy", None, None),
        P("dx", "dy", None),
    ) + (whole,) * 7
    return jax.shard_map(
        shards, mesh=mesh, in_specs=placed, out_specs=P("dx", "dy", None, None), check_vma=False
    )
```
